512 devices in a mesh: dp: 16 (over z_lo, core), expert: 32 (over y, x, z_hi).
Axes of the slice: x: 4, y: 4, z: 16 (z_hi: 2, z_lo: 8; z = z_hi * 8 + z_lo), core: 2. Of those that a mesh axis runs over, the one named last changes fastest.
Arguments:
- tokens: bfloat16 [4096, 4096], P('expert', 'dp'), may hold values from -6 to 6
- routes: int32 [4096, 2], P('expert'), may hold values from 0 to 31, as said below
- route_weights: float32 [4096, 2], P('expert'), may hold values from 0.05 to 0.5
- cotangent: bfloat16 [4096, 4096], P('expert', 'dp'), may hold values from -6 to 6
- w_gate_up: bfloat16 [32, 4096, 2048], P('expert', 'dp'), may hold values from -0.09375 to 0.09375
- w_down: bfloat16 [32, 1024, 4096], P('expert', None, 'dp'), may hold values from -0.1875 to 0.1875
Outputs:
- mixed: bfloat16 [4096, 4096], P('expert', 'dp')
- token_grad: bfloat16 [4096, 4096], P('expert', 'dp')
- grad_gate_up: bfloat16 [32, 4096, 2048], P('expert', 'dp')
- grad_down: bfloat16 [32, 1024, 4096], P('expert', None, 'dp')
The draws below stay inside these ranges and needn't reach their ends.
Inputs may be any that keep to these rules, and one draw needn't show every extreme that they name: Each row names 2 different experts. One expert, the same for all rows, is named by exactly 16 routes in each aligned block of 128 rows (the rows of one device); in each such block every other expert is named by at most 8 routes, their counts differ by at most one, and some reach 8.
All inputs are finite; a program needn't handle non-finite values.
Results may differ from the reference program's by a relative error of at most 0.035.
Values may be sent and summed in bfloat16 or wider, within the bound.
No kernel may reach another device: no remote copies, remote signals or barrier semaphores. Data moves between devices by JAX's collectives and lax.ppermute only.
A program may use at most 64 MiB of HBM per device.

```python
import jax
import jax.numpy as jnp
from jax import lax

D = 4096
F = 1024
TOK_DEV = 128
TOP = 2
EXPERTS = 32
CAP = 16
TOKENS = 4096
N_DP = 16


def draw_routes(key, part):
    key = jax.random.fold_in(key, 11)
    hot_key, rest_key = jax.random.split(key)
    busiest = jax.random.randint(hot_key, (), 0, EXPERTS).astype(jnp.int32)
    block_keys = jax.random.split(rest_key, TOKENS // TOK_DEV)

    def one_block(block_key):
        key_a, key_b, key_c, key_d = jax.random.split(block_key, 4)
        order = jax.random.permutation(key_a, TOK_DEV)
        hot_token = order < CAP
        hot_slot = jax.random.randint(key_b, (TOK_DEV,), 0, TOP)
        is_hot = hot_token[:, None] & (jnp.arange(TOP, dtype=jnp.int32)[None, :] == hot_slot[:, None])
        flat_hot = is_hot.reshape(-1)
        cold_flag = 1 - flat_hot.astype(jnp.int32)
        ordinal = jnp.cumsum(cold_flag) - cold_flag
        cycle = jax.random.permutation(key_c, EXPERTS - 1).astype(jnp.int32)
        cold_ids = cycle + (cycle >= busiest).astype(jnp.int32)
        offset = jax.random.randint(key_d, (), 0, EXPERTS - 1)
        picked = cold_ids[(ordinal + offset) % (EXPERTS - 1)]
        return jnp.where(flat_hot, busiest, picked).reshape(TOK_DEV, TOP).astype(jnp.int32)
    return jax.vmap(one_block)(block_keys).reshape(TOKENS, TOP)


def block_scale(own_key, extent, cuts, smallest, top_value):
    factor_of, own = 1.0, jax.random.fold_in(own_key, 6)
    for dim, shards_of in cuts:
        steps = jnp.exp(jax.random.uniform(jax.random.fold_in(own, dim), (shards_of,), jnp.float32, smallest / len(cuts), top_value / len(cuts)))
        factor_of = factor_of * jnp.repeat(steps, extent[dim] // shards_of).reshape([-1 if axis == dim else 1 for axis in range(len(extent))])
    return factor_of


def noise(key, extent, spread, limit, cuts=(), held_as=jnp.bfloat16):
    result = spread * jax.random.normal(key, extent, jnp.float32)
    if cuts:
        result = result * block_scale(key, extent, cuts, -0.22, 0.18)
    return jnp.clip(result, -limit, limit).astype(held_as)


def setup_inputs(seed: int = 0) -> dict:
    keys = jax.random.split(jax.random.key(seed), 7)
    tokens = noise(keys[0], (TOKENS, D), 1.0, 6.0, ((0, 32), (1, 16)))
    routes = draw_routes(jax.random.fold_in(keys[6], 71), 0)
    route_weights = jnp.clip(0.05 + 0.45 * jax.random.uniform(keys[2], (TOKENS, TOP), jnp.float32) ** block_scale(keys[2], (TOKENS, TOP), ((0, 32),), -0.2, 0.2), 0.05, 0.5)
    cotangent = noise(keys[3], (TOKENS, D), 1.0, 6.0, ((0, 32), (1, 16)))
    w_gate_up = noise(keys[4], (EXPERTS, D, 2 * F), D ** -0.5, 0.09375, ((0, 32), (1, 16)))
    w_down = noise(keys[5], (EXPERTS, F, D), F ** -0.5, 0.1875, ((0, 32), (2, 16)))
    return {"tokens": tokens, "routes": routes, "route_weights": route_weights, "cotangent": cotangent, "w_gate_up": w_gate_up, "w_down": w_down}


def block_rounded(rows, weight_blocks):
    count = rows.shape[0]
    pieces = rows.reshape(count, N_DP, D // N_DP).astype(jnp.float32)
    terms = jnp.einsum('rnd,ndf->rnf', pieces, weight_blocks.astype(jnp.float32))
    terms = lax.optimization_barrier(terms.astype(jnp.bfloat16))
    return jnp.sum(terms.astype(jnp.float32), axis=1)


def reference(tokens, routes, route_weights, cotangent, w_gate_up, w_down):
    per_block = TOK_DEV * TOP
    total_routes = TOKENS * TOP
    flat = routes.reshape(EXPERTS, per_block)
    expert_ids = jnp.arange(EXPERTS, dtype=jnp.int32)
    onehot = (flat[:, :, None] == expert_ids[None, None, :]).astype(jnp.int32)
    rank = jnp.cumsum(onehot, axis=1) - onehot
    slot_of = jnp.sum(rank * onehot, axis=2)
    block_of = jnp.arange(EXPERTS, dtype=jnp.int32)[:, None] + jnp.zeros_like(flat)
    route_ids = jnp.arange(total_routes, dtype=jnp.int32).reshape(EXPERTS, per_block)
    table = jnp.full((EXPERTS, EXPERTS * CAP), total_routes, jnp.int32)
    table = table.at[flat, block_of * CAP + slot_of].set(route_ids)
    x_route = jnp.concatenate([jnp.repeat(tokens, TOP, axis=0), jnp.zeros((1, D), jnp.bfloat16)], axis=0)
    g_vals = route_weights.reshape(-1, 1) * jnp.repeat(cotangent.astype(jnp.float32), TOP, axis=0)
    g_route = jnp.concatenate([g_vals.astype(jnp.bfloat16), jnp.zeros((1, D), jnp.bfloat16)], axis=0)

    def one_expert(inputs):
        index, gate_up_w, down_w = inputs
        x_rows = x_route[index]
        g_rows = g_route[index]
        sums = block_rounded(x_rows, gate_up_w.reshape(N_DP, D // N_DP, 2 * F))
        gate = sums[:, :F]
        up = sums[:, F:]
        hidden = (jax.nn.silu(gate) * up).astype(jnp.bfloat16)
        expert_out = jnp.dot(hidden, down_w, preferred_element_type=jnp.float32).astype(jnp.bfloat16)
        down_blocks = jnp.transpose(down_w.reshape(F, N_DP, D // N_DP), (1, 2, 0))
        hidden_grad = block_rounded(g_rows, down_blocks)
        sig = jax.nn.sigmoid(gate)
        dgate = hidden_grad * up * sig * (1.0 + gate * (1.0 - sig))
        dup = hidden_grad * (gate * sig)
        gate_up_grad = jnp.concatenate([dgate, dup], axis=1).astype(jnp.bfloat16)
        route_grad = jnp.dot(gate_up_grad, gate_up_w.T, preferred_element_type=jnp.float32).astype(jnp.bfloat16)
        grad_gu = jnp.dot(x_rows.T, gate_up_grad, preferred_element_type=jnp.float32).astype(jnp.bfloat16)
        grad_dn = jnp.dot(hidden.T, g_rows, preferred_element_type=jnp.float32).astype(jnp.bfloat16)
        return expert_out, route_grad, grad_gu, grad_dn

    outs, rgrads, grad_gate_up, grad_down = lax.map(one_expert, (table, w_gate_up, w_down))
    where = table.reshape(-1)
    y_routes = jnp.zeros((total_routes + 1, D), jnp.float32).at[where].add(outs.reshape(-1, D).astype(jnp.float32))
    dx_routes = jnp.zeros((total_routes + 1, D), jnp.float32).at[where].add(rgrads.reshape(-1, D).astype(jnp.float32))
    weighted = y_routes[:total_routes] * route_weights.reshape(-1, 1)
    mixed = jnp.sum(weighted.reshape(TOKENS, TOP, D), axis=1).astype(jnp.bfloat16)
    token_grad = jnp.sum(dx_routes[:total_routes].reshape(TOKENS, TOP, D), axis=1).astype(jnp.bfloat16)
    return mixed, token_grad, grad_gate_up, grad_down
```

```python
import jax
import jax.numpy as jnp
from jax import lax
from jax.sharding import PartitionSpec as P

BF = jnp.bfloat16
F32 = jnp.float32


def mm(a, b):
    return jnp.dot(a, b, preferred_element_type=F32)


def mm_nt(a, b):
    return lax.dot_general(a, b, (((1,), (1,)), ((), ())), preferred_element_type=F32)


def mm_tn(a, b):
    return lax.dot_general(a, b, (((0,), (0,)), ((), ())), preferred_element_type=F32)


def roll_rows(rows, shift):
    twice = jnp.concatenate([rows, rows], axis=0)
    return lax.dynamic_slice_in_dim(twice, shift, rows.shape[0], axis=0)


def route_slots(routes_t, experts, slots):
    top, count = routes_t.shape
    ids = lax.broadcasted_iota(jnp.int32, (experts, count), 0)
    earlier = lax.broadcasted_iota(jnp.int32, (count, count), 0) < lax.broadcasted_iota(
        jnp.int32, (count, count), 1
    )
    earlier = earlier.astype(BF)
    before = jnp.zeros((experts, 1), F32)
    targets = []
    for k in range(top):
        named = ids == routes_t[k : k + 1]
        hot = named.astype(BF)
        rank = mm(hot, earlier) + before
        slot = jnp.sum(jnp.where(named, rank, 0.0), axis=0, keepdims=True)
        targets.append(routes_t[k : k + 1] * slots + slot.astype(jnp.int32))
        before = before + jnp.sum(hot.astype(F32), axis=1, keepdims=True)
    return targets


def on_device(tokens, routes, route_weights, cotangent, w_gate_up, w_down):
    experts = lax.axis_size("expert")
    n_dp = lax.axis_size("dp")
    chips = n_dp // 2
    tok_rows, feat = tokens.shape
    top = routes.shape[1]
    width = w_down.shape[1]
    slots = 2 * tok_rows * top // experts
    rows = experts * slots
    half = rows // 2
    step = half // chips
    me = lax.axis_index("dp")
    chip = me // 2
    core = me % 2
    gu = w_gate_up[0]
    down = w_down[0]

    targets = route_slots(routes.T, experts, slots)
    weights = route_weights.T
    slot_ids = lax.broadcasted_iota(jnp.int32, (rows, tok_rows), 0)
    picked = [slot_ids == target for target in targets]
    selector = sum(p.astype(BF) for p in picked)
    slot_weight = sum(
        jnp.sum(jnp.where(p, weights[k : k + 1], 0.0), axis=1, keepdims=True)
        for k, p in enumerate(picked)
    )
    send_x = mm(selector, tokens).astype(BF)
    send_g = (mm(selector, cotangent) * slot_weight).astype(BF)
    send = jnp.concatenate([send_x, send_g], axis=1).reshape(experts, slots, 2 * feat)
    recv = lax.all_to_all(send, "expert", split_axis=0, concat_axis=0, tiled=True)

    both = recv.reshape(2, half, 2 * feat)
    mine = roll_rows(lax.dynamic_index_in_dim(both, core, 0, keepdims=False), chip * step)
    theirs = roll_rows(lax.dynamic_index_in_dim(both, 1 - core, 0, keepdims=False), chip * step)

    def terms(xg):
        return jnp.concatenate(
            [mm(xg[:, :feat], gu).astype(BF), mm_nt(xg[:, feat:], down).astype(BF)], axis=1
        )

    pair = [(i, i ^ 1) for i in range(n_dp)]
    right = [(i, i + 2) for i in range(n_dp - 2)]
    left = [(i + 2, i) for i in range(n_dp - 2)]
    from_pair = lax.ppermute(terms(theirs), "dp", pair)
    part = (terms(mine).astype(F32) + from_pair.astype(F32)).astype(BF).reshape(chips, step, -1)

    go_right, go_left = part[chips - 1], part[1]
    for s in range(chips - 1):
        got_r = lax.ppermute(go_right, "dp", right)
        got_l = lax.ppermute(go_left, "dp", left)
        if s < chips - 2:
            go_right = (got_r.astype(F32) + part[chips - 2 - s].astype(F32)).astype(BF)
            go_left = (got_l.astype(F32) + part[2 + s].astype(F32)).astype(BF)
    sums = got_r.astype(F32) + got_l.astype(F32) + part[0].astype(F32)

    gate = sums[:, :width]
    up = sums[:, width : 2 * width]
    hidden_grad = sums[:, 2 * width :]
    sig = jax.nn.sigmoid(gate)
    silu_vals = gate * sig
    own = jnp.concatenate(
        [
            (silu_vals * up).astype(BF),
            (hidden_grad * up * sig * (1.0 + gate * (1.0 - sig))).astype(BF),
            (hidden_grad * silu_vals).astype(BF),
        ],
        axis=1,
    )

    rights, lefts = [], []
    go_right = go_left = own
    for s in range(chips - 1):
        go_right = lax.ppermute(go_right, "dp", right)
        go_left = lax.ppermute(go_left, "dp", left)
        rights.append(go_right)
        lefts.append(go_left)
    pieces = [own]
    for m in range(1, chips):
        pieces.append(jnp.where(chip + m < chips, lefts[m - 1], rights[chips - 1 - m]))
    act_mine = jnp.concatenate(pieces, axis=0)
    act_theirs = lax.ppermute(act_mine, "dp", pair)

    def outputs(act):
        return jnp.concatenate(
            [
                mm(act[:, :width], down).astype(BF),
                mm_nt(act[:, width:], gu).astype(BF),
            ],
            axis=1,
        )

    back = [roll_rows(outputs(a), half - chip * step) for a in (act_mine, act_theirs)]
    first = jnp.where(core == 0, back[0], back[1])
    second = jnp.where(core == 0, back[1], back[0])
    back = jnp.concatenate([first, second], axis=0).reshape(experts, slots, 2 * feat)
    ret = lax.all_to_all(back, "expert", split_axis=0, concat_axis=0, tiled=True)
    ret = ret.reshape(rows, 2 * feat)

    act = jnp.concatenate([act_mine, act_theirs], axis=0)
    xg = jnp.concatenate([mine, theirs], axis=0)
    grad_gu = mm_tn(xg[:, :feat], act[:, width:]).astype(BF)
    grad_dn = mm_tn(act[:, :width], xg[:, feat:]).astype(BF)

    mixed = sum(
        mm_tn(p.astype(BF), ret[:, :feat]) * route_weights[:, k : k + 1]
        for k, p in enumerate(picked)
    ).astype(BF)
    token_grad = mm_tn(selector, ret[:, feat:]).astype(BF)
    return (mixed, token_grad, grad_gu[None], grad_dn[None])


def solution(mesh):
    return jax.shard_map(
        on_device,
        mesh=mesh,
        in_specs=(
            P("expert", "dp"),
            P("expert", None),
            P("expert", None),
            P("expert", "dp"),
            P("expert", "dp", None),
            P("expert", None, "dp"),
        ),
        out_specs=(
            P("expert", "dp"),
            P("expert", "dp"),
            P("expert", "dp", None),
            P("expert", None, "dp"),
        ),
        check_vma=False,
    )
```

```python
import jax
import jax.numpy as jnp
from jax import lax
from jax.sharding import PartitionSpec as P

BF = jnp.bfloat16
F32 = jnp.float32


def mm(a, b):
    return jnp.dot(a, b, preferred_element_type=F32)


def mm_nt(a, b):
    return lax.dot_general(a, b, (((1,), (1,)), ((), ())), preferred_element_type=F32)


def mm_tn(a, b):
    return lax.dot_general(a, b, (((0,), (0,)), ((), ())), preferred_element_type=F32)


def route_slots(routes_t, experts, slots):
    top, count = routes_t.shape
    ids = lax.broadcasted_iota(jnp.int32, (experts, count), 0)
    earlier = lax.broadcasted_iota(jnp.int32, (count, count), 0) < lax.broadcasted_iota(
        jnp.int32, (count, count), 1
    )
    earlier = earlier.astype(BF)
    before = jnp.zeros((experts, 1), F32)
    targets = []
    for k in range(top):
        named = ids == routes_t[k : k + 1]
        hot = named.astype(BF)
        rank = mm(hot, earlier) + before
        slot = jnp.sum(jnp.where(named, rank, 0.0), axis=0, keepdims=True)
        targets.append(routes_t[k : k + 1] * slots + slot.astype(jnp.int32))
        before = before + jnp.sum(hot.astype(F32), axis=1, keepdims=True)
    return targets


def on_device(tokens, routes, route_weights, cotangent, w_gate_up, w_down):
    experts = lax.axis_size("expert")
    n_dp = lax.axis_size("dp")
    chips = n_dp // 2
    tok_rows, feat = tokens.shape
    top = routes.shape[1]
    width = w_down.shape[1]
    slots = 2 * tok_rows * top // experts
    rows = experts * slots
    half = rows // 2
    step = half // chips
    me = lax.axis_index("dp")
    chip = me // 2
    core = me % 2
    gu = w_gate_up[0]
    down = w_down[0]

    targets = route_slots(routes.T, experts, slots)
    weights = route_weights.T
    slot_ids = lax.broadcasted_iota(jnp.int32, (rows, tok_rows), 0)
    picked = [slot_ids == target for target in targets]
    selector = sum(p.astype(BF) for p in picked)
    slot_weight = sum(
        jnp.sum(jnp.where(p, weights[k : k + 1], 0.0), axis=1, keepdims=True)
        for k, p in enumerate(picked)
    )
    send_x = mm(selector, tokens).astype(BF)
    send_g = (mm(selector, cotangent) * slot_weight).astype(BF)
    send = jnp.concatenate([send_x, send_g], axis=1).reshape(experts, slots, 2 * feat)
    recv = lax.all_to_all(send, "expert", split_axis=0, concat_axis=0, tiled=True)

    def flip(rows_):
        blocks = rows_.reshape((2, 2, 2, 2, step) + rows_.shape[1:])
        for axis, bit in enumerate((core, chip % 2, chip // 2 % 2, chip // 4)):
            blocks = jnp.where(bit == 1, jnp.flip(blocks, axis), blocks)
        return blocks.reshape(rows_.shape)

    stages = [
        [(i, i ^ bit) for i in range(n_dp)] for bit in (1, 2, 4, 8)
    ]
    xg = flip(recv.reshape(rows, 2 * feat))
    x_rows, g_rows = xg[:, :feat], xg[:, feat:]

    def split(mul, left_rows, weight):
        return mul(left_rows[half:], weight).astype(BF), mul(left_rows[:half], weight)

    def reduce_scatter(mul, left_rows, weight):
        away, keep = split(mul, left_rows, weight)
        for n, perm in enumerate(stages):
            keep = lax.ppermute(away, "dp", perm).astype(F32) + keep.astype(F32)
            if n + 1 < len(stages):
                middle = keep.shape[0] // 2
                away, keep = keep[middle:].astype(BF), keep[:middle].astype(BF)
        return keep

    def all_gather(own):
        for perm in stages[::-1]:
            own = jnp.concatenate([own, lax.ppermute(own, "dp", perm)], axis=0)
        return own

    gate_up = reduce_scatter(mm, x_rows, gu)
    hidden_grad = reduce_scatter(mm_nt, g_rows, down)
    gate = gate_up[:, :width]
    up = gate_up[:, width:]
    sig = jax.nn.sigmoid(gate)
    silu_vals = gate * sig
    hidden = all_gather((silu_vals * up).astype(BF))
    dgate = hidden_grad * up * sig * (1.0 + gate * (1.0 - sig))
    dup = hidden_grad * silu_vals
    gate_up_grad = all_gather(jnp.concatenate([dgate, dup], axis=1).astype(BF))

    back = jnp.concatenate(
        [mm(hidden, down).astype(BF), mm_nt(gate_up_grad, gu).astype(BF)], axis=1
    )
    back = flip(back).reshape(experts, slots, 2 * feat)
    ret = lax.all_to_all(back, "expert", split_axis=0, concat_axis=0, tiled=True)
    ret = ret.reshape(rows, 2 * feat)
    grad_gu = mm_tn(x_rows, gate_up_grad).astype(BF)
    grad_dn = mm_tn(hidden, g_rows).astype(BF)

    mixed = sum(
        mm_tn(p.astype(BF), ret[:, :feat]) * route_weights[:, k : k + 1]
        for k, p in enumerate(picked)
    ).astype(BF)
    token_grad = mm_tn(selector, ret[:, feat:]).astype(BF)
    return (mixed, token_grad, grad_gu[None], grad_dn[None])


def solution(mesh):
    return jax.shard_map(
        on_device,
        mesh=mesh,
        in_specs=(
            P("expert", "dp"),
            P("expert", None),
            P("expert", None),
            P("expert", "dp"),
            P("expert", "dp", None),
            P("expert", None, "dp"),
        ),
        out_specs=(
            P("expert", "dp"),
            P("expert", "dp"),
            P("expert", "dp", None),
            P("expert", None, "dp"),
        ),
        check_vma=False,
    )
```

```python
import jax
import jax.numpy as jnp
from jax import lax
from jax.sharding import PartitionSpec as P

BF = jnp.bfloat16
F32 = jnp.float32


def mm(a, b):
    return jnp.dot(a, b, preferred_element_type=F32)


def mm_nt(a, b):
    return lax.dot_general(a, b, (((1,), (1,)), ((), ())), preferred_element_type=F32)


def mm_tn(a, b):
    return lax.dot_general(a, b, (((0,), (0,)), ((), ())), preferred_element_type=F32)


def route_slots(routes_t, experts, slots):
    top, count = routes_t.shape
    ids = lax.broadcasted_iota(jnp.int32, (experts, count), 0)
    earlier = lax.broadcasted_iota(jnp.int32, (count, count), 0) < lax.broadcasted_iota(
        jnp.int32, (count, count), 1
    )
    earlier = earlier.astype(BF)
    before = jnp.zeros((experts, 1), F32)
    targets = []
    for k in range(top):
        named = ids == routes_t[k : k + 1]
        hot = named.astype(BF)
        rank = mm(hot, earlier) + before
        slot = jnp.sum(jnp.where(named, rank, 0.0), axis=0, keepdims=True)
        slot = slot.astype(jnp.int32)
        targets.append(
            jnp.where(
                slot < slots, routes_t[k : k + 1] * slots + slot, (experts - 1) * slots + slot
            )
        )
        before = before + jnp.sum(hot.astype(F32), axis=1, keepdims=True)
    column = lax.broadcasted_iota(jnp.int32, (experts, 1), 0)
    busiest = jnp.sum(jnp.where(before > slots, column, 0))
    return targets, busiest


def on_device(tokens, routes, route_weights, cotangent, w_gate_up, w_down):
    experts = lax.axis_size("expert")
    n_dp = lax.axis_size("dp")
    chips = n_dp // 2
    tok_rows, feat = tokens.shape
    top = routes.shape[1]
    width = w_down.shape[1]
    slots = tok_rows * top // experts
    rows = 2 * experts * slots
    sent = (experts + 1) * slots
    half = rows // 2
    step = half // chips
    me = lax.axis_index("dp")
    chip = me // 2
    core = me % 2
    gu = w_gate_up[0]
    down = w_down[0]

    targets, busiest = route_slots(routes.T, experts, slots)
    weights = route_weights.T
    slot_ids = lax.broadcasted_iota(jnp.int32, (sent, tok_rows), 0)
    picked = [slot_ids == target for target in targets]
    selector = sum(p.astype(BF) for p in picked)
    slot_weight = sum(
        jnp.sum(jnp.where(p, weights[k : k + 1], 0.0), axis=1, keepdims=True)
        for k, p in enumerate(picked)
    )
    send_x = mm(selector, tokens).astype(BF)
    send_g = (mm(selector, cotangent) * slot_weight).astype(BF)
    send = jnp.concatenate([send_x, send_g], axis=1)

    def exchange(blocks):
        blocks = blocks.reshape(experts, slots, 2 * feat)
        blocks = lax.all_to_all(blocks, "expert", split_axis=0, concat_axis=0, tiled=True)
        return blocks.reshape(experts * slots, 2 * feat)

    owner = lax.axis_index("expert")
    doubling = [[(i, i ^ (1 << k)) for i in range(experts)] for k in range(experts.bit_length() - 1)]
    recv = exchange(send[: experts * slots])
    more = send[experts * slots :]
    for perm in doubling:
        more = jnp.concatenate([more, lax.ppermute(more, "expert", perm)], axis=0)
    recv = jnp.concatenate([recv, jnp.where(owner == busiest, more, jnp.zeros_like(more))], axis=0)

    def flip(rows_):
        blocks = rows_.reshape((2, 2, 2, 2, step) + rows_.shape[1:])
        for axis, bit in enumerate((core, chip % 2, chip // 2 % 2, chip // 4)):
            blocks = jnp.where(bit == 1, jnp.flip(blocks, axis), blocks)
        return blocks.reshape(rows_.shape)

    stages = [
        [(i, i ^ bit) for i in range(n_dp)] for bit in (1, 2, 4, 8)
    ]
    xg = flip(recv)
    x_rows, g_rows = xg[:, :feat], xg[:, feat:]

    def split(mul, left_rows, weight):
        return mul(left_rows[half:], weight).astype(BF), mul(left_rows[:half], weight)

    def reduce_scatter(mul, left_rows, weight):
        away, keep = split(mul, left_rows, weight)
        for n, perm in enumerate(stages):
            keep = lax.ppermute(away, "dp", perm).astype(F32) + keep.astype(F32)
            if n + 1 < len(stages):
                middle = keep.shape[0] // 2
                away, keep = keep[middle:].astype(BF), keep[:middle].astype(BF)
        return keep

    def all_gather(own):
        for perm in stages[::-1]:
            own = jnp.concatenate([own, lax.ppermute(own, "dp", perm)], axis=0)
        return own

    gate_up = reduce_scatter(mm, x_rows, gu)
    hidden_grad = reduce_scatter(mm_nt, g_rows, down)
    gate = gate_up[:, :width]
    up = gate_up[:, width:]
    sig = jax.nn.sigmoid(gate)
    silu_vals = gate * sig
    hidden = all_gather((silu_vals * up).astype(BF))
    dgate = hidden_grad * up * sig * (1.0 + gate * (1.0 - sig))
    dup = hidden_grad * silu_vals
    gate_up_grad = all_gather(jnp.concatenate([dgate, dup], axis=1).astype(BF))

    back = jnp.concatenate(
        [mm(hidden, down).astype(BF), mm_nt(gate_up_grad, gu).astype(BF)], axis=1
    )
    back = flip(back)
    ret = exchange(back[: experts * slots])
    more = back[experts * slots :]
    for k, perm in reversed(list(enumerate(doubling))):
        middle = more.shape[0] // 2
        got = lax.ppermute(more[middle:], "expert", perm)
        more = jnp.where(((owner ^ busiest) >> k) & 1 == 1, got, more[:middle])
    ret = jnp.concatenate([ret, more], axis=0)
    grad_gu = mm_tn(x_rows, gate_up_grad).astype(BF)
    grad_dn = mm_tn(hidden, g_rows).astype(BF)

    mixed = sum(
        mm_tn(p.astype(BF), ret[:, :feat]) * route_weights[:, k : k + 1]
        for k, p in enumerate(picked)
    ).astype(BF)
    token_grad = mm_tn(selector, ret[:, feat:]).astype(BF)
    return (mixed, token_grad, grad_gu[None], grad_dn[None])


def solution(mesh):
    return jax.shard_map(
        on_device,
        mesh=mesh,
        in_specs=(
            P("expert", "dp"),
            P("expert", None),
            P("expert", None),
            P("expert", "dp"),
            P("expert", "dp", None),
            P("expert", None, "dp"),
        ),
        out_specs=(
            P("expert", "dp"),
            P("expert", "dp"),
            P("expert", "dp", None),
            P("expert", None, "dp"),
        ),
        check_vma=False,
    )
```

```python
import jax
import jax.numpy as jnp
from jax import lax
from jax.sharding import PartitionSpec as P

BF = jnp.bfloat16
F32 = jnp.float32


def mm(a, b):
    return jnp.dot(a, b, preferred_element_type=F32)


def mm_nt(a, b):
    return lax.dot_general(a, b, (((1,), (1,)), ((), ())), preferred_element_type=F32)


def mm_tn(a, b):
    return lax.dot_general(a, b, (((0,), (0,)), ((), ())), preferred_element_type=F32)


def route_slots(routes_t, experts, slots):
    top, count = routes_t.shape
    ids = lax.broadcasted_iota(jnp.int32, (experts, count), 0)
    earlier = lax.broadcasted_iota(jnp.int32, (count, count), 0) < lax.broadcasted_iota(
        jnp.int32, (count, count), 1
    )
    earlier = earlier.astype(BF)
    before = jnp.zeros((experts, 1), F32)
    targets = []
    for k in range(top):
        named = ids == routes_t[k : k + 1]
        hot = named.astype(BF)
        rank = mm(hot, earlier) + before
        slot = jnp.sum(jnp.where(named, rank, 0.0), axis=0, keepdims=True)
        slot = slot.astype(jnp.int32)
        targets.append(
            jnp.where(
                slot < slots, routes_t[k : k + 1] * slots + slot, (experts - 1) * slots + slot
            )
        )
        before = before + jnp.sum(hot.astype(F32), axis=1, keepdims=True)
    column = lax.broadcasted_iota(jnp.int32, (experts, 1), 0)
    busiest = jnp.sum(jnp.where(before > slots, column, 0))
    return targets, busiest


def on_device(tokens, routes, route_weights, cotangent, w_gate_up, w_down):
    experts = lax.axis_size("expert")
    n_dp = lax.axis_size("dp")
    chips = n_dp // 2
    tok_rows, feat = tokens.shape
    top = routes.shape[1]
    width = w_down.shape[1]
    slots = tok_rows * top // experts
    rows = 2 * experts * slots
    sent = (experts + 1) * slots
    half = rows // 2
    step = half // chips
    me = lax.axis_index("dp")
    chip = me // 2
    core = me % 2
    gu = w_gate_up[0]
    down = w_down[0]

    targets, busiest = route_slots(routes.T, experts, slots)
    weights = route_weights.T
    slot_ids = lax.broadcasted_iota(jnp.int32, (sent, tok_rows), 0)
    picked = [slot_ids == target for target in targets]
    selector = sum(p.astype(BF) for p in picked)
    slot_weight = sum(
        jnp.sum(jnp.where(p, weights[k : k + 1], 0.0), axis=1, keepdims=True)
        for k, p in enumerate(picked)
    )
    send_x = mm(selector, tokens).astype(BF)
    send_g = (mm(selector, cotangent) * slot_weight).astype(BF)
    send = jnp.concatenate([send_x, send_g], axis=1)

    def exchange(blocks):
        blocks = blocks.reshape(experts, slots, 2 * feat)
        blocks = lax.all_to_all(blocks, "expert", split_axis=0, concat_axis=0, tiled=True)
        return blocks.reshape(experts * slots, 2 * feat)

    owner = lax.axis_index("expert")
    digits = [(1, 2), (2, 4), (8, experts // 8)]

    def digit(number, place, base):
        return number // place % base

    shifts = [
        [
            [(i, i + place * ((digit(i, place, base) + d) % base - digit(i, place, base))) for i in range(experts)]
            for d in range(1, base)
        ]
        for place, base in digits
    ]
    recv = exchange(send[: experts * slots])
    more = send[experts * slots :]
    for perms in shifts:
        more = jnp.concatenate([more] + [lax.ppermute(more, "expert", p) for p in perms], axis=0)
    recv = jnp.concatenate([recv, jnp.where(owner == busiest, more, jnp.zeros_like(more))], axis=0)

    def flip(rows_):
        blocks = rows_.reshape((2, 2, 2, 2, step) + rows_.shape[1:])
        for axis, bit in enumerate((core, chip % 2, chip // 2 % 2, chip // 4)):
            blocks = jnp.where(bit == 1, jnp.flip(blocks, axis), blocks)
        return blocks.reshape(rows_.shape)

    stages = [
        [(i, i ^ bit) for i in range(n_dp)] for bit in (1, 2, 4, 8)
    ]
    xg = flip(recv)
    x_rows, g_rows = xg[:, :feat], xg[:, feat:]

    def split(mul, left_rows, weight):
        return mul(left_rows[half:], weight).astype(BF), mul(left_rows[:half], weight)

    def reduce_scatter(mul, left_rows, weight):
        away, keep = split(mul, left_rows, weight)
        for n, perm in enumerate(stages):
            keep = lax.ppermute(away, "dp", perm).astype(F32) + keep.astype(F32)
            if n + 1 < len(stages):
                middle = keep.shape[0] // 2
                away, keep = keep[middle:].astype(BF), keep[:middle].astype(BF)
        return keep

    def all_gather(own):
        for perm in stages[::-1]:
            own = jnp.concatenate([own, lax.ppermute(own, "dp", perm)], axis=0)
        return own

    gate_up = reduce_scatter(mm, x_rows, gu)
    hidden_grad = reduce_scatter(mm_nt, g_rows, down)
    gate = gate_up[:, :width]
    up = gate_up[:, width:]
    sig = jax.nn.sigmoid(gate)
    silu_vals = gate * sig
    hidden = all_gather((silu_vals * up).astype(BF))
    dgate = hidden_grad * up * sig * (1.0 + gate * (1.0 - sig))
    dup = hidden_grad * silu_vals
    gate_up_grad = all_gather(jnp.concatenate([dgate, dup], axis=1).astype(BF))

    back = jnp.concatenate(
        [mm(hidden, down).astype(BF), mm_nt(gate_up_grad, gu).astype(BF)], axis=1
    )
    back = flip(back)
    ret = exchange(back[: experts * slots])
    more = back[experts * slots :]
    for (place, base), perms in zip(digits[::-1], shifts[::-1]):
        parts = more.reshape(base, -1, 2 * feat)
        behind = (digit(busiest, place, base) - digit(owner, place, base)) % base
        more = parts[0]
        for d in range(1, base):
            got = lax.ppermute(parts[d], "expert", perms[base - d - 1])
            more = jnp.where(behind == d, got, more)
    ret = jnp.concatenate([ret, more], axis=0)
    grad_gu = mm_tn(x_rows, gate_up_grad).astype(BF)
    grad_dn = mm_tn(hidden, g_rows).astype(BF)

    mixed = sum(
        mm_tn(p.astype(BF), ret[:, :feat]) * route_weights[:, k : k + 1]
        for k, p in enumerate(picked)
    ).astype(BF)
    token_grad = mm_tn(selector, ret[:, feat:]).astype(BF)
    return (mixed, token_grad, grad_gu[None], grad_dn[None])


def solution(mesh):
    return jax.shard_map(
        on_device,
        mesh=mesh,
        in_specs=(
            P("expert", "dp"),
            P("expert", None),
            P("expert", None),
            P("expert", "dp"),
            P("expert", "dp", None),
            P("expert", None, "dp"),
        ),
        out_specs=(
            P("expert", "dp"),
            P("expert", "dp"),
            P("expert", "dp", None),
            P("expert", None, "dp"),
        ),
        check_vma=False,
    )
```

```python
import jax
import jax.numpy as jnp
from jax import lax
from jax.sharding import PartitionSpec as P

BF = jnp.bfloat16
F32 = jnp.float32


def mm(a, b):
    return jnp.dot(a, b, preferred_element_type=F32)


def mm_nt(a, b):
    return lax.dot_general(a, b, (((1,), (1,)), ((), ())), preferred_element_type=F32)


def mm_tn(a, b):
    return lax.dot_general(a, b, (((0,), (0,)), ((), ())), preferred_element_type=F32)


def route_slots(routes_t, experts, slots):
    top, count = routes_t.shape
    ids = lax.broadcasted_iota(jnp.int32, (experts, count), 0)
    earlier = lax.broadcasted_iota(jnp.int32, (count, count), 0) < lax.broadcasted_iota(
        jnp.int32, (count, count), 1
    )
    earlier = earlier.astype(BF)
    before = jnp.zeros((experts, 1), F32)
    targets = []
    for k in range(top):
        named = ids == routes_t[k : k + 1]
        hot = named.astype(BF)
        rank = mm(hot, earlier) + before
        slot = jnp.sum(jnp.where(named, rank, 0.0), axis=0, keepdims=True)
        targets.append(routes_t[k : k + 1] * slots + slot.astype(jnp.int32))
        before = before + jnp.sum(hot.astype(F32), axis=1, keepdims=True)
    return targets


def on_device(tokens, routes, route_weights, cotangent, w_gate_up, w_down):
    experts = lax.axis_size("expert")
    n_dp = lax.axis_size("dp")
    chips = n_dp // 2
    tok_rows, feat = tokens.shape
    top = routes.shape[1]
    width = w_down.shape[1]
    slots = 2 * tok_rows * top // experts
    rows = experts * slots
    half = rows // 2
    step = half // chips
    me = lax.axis_index("dp")
    chip = me // 2
    core = me % 2
    gu = w_gate_up[0]
    down = w_down[0]

    targets = route_slots(routes.T, experts, slots)
    weights = route_weights.T
    slot_ids = lax.broadcasted_iota(jnp.int32, (rows, tok_rows), 0)
    picked = [slot_ids == target for target in targets]
    selector = sum(p.astype(BF) for p in picked)
    slot_weight = sum(
        jnp.sum(jnp.where(p, weights[k : k + 1], 0.0), axis=1, keepdims=True)
        for k, p in enumerate(picked)
    )
    send_x = mm(selector, tokens).astype(BF)
    send_g = (mm(selector, cotangent) * slot_weight).astype(BF)
    send = jnp.concatenate([send_x, send_g], axis=1).reshape(experts, slots, 2 * feat)
    recv = lax.all_to_all(send, "expert", split_axis=0, concat_axis=0, tiled=True)

    def flip(rows_):
        blocks = rows_.reshape((2, 2, 2, 2, step) + rows_.shape[1:])
        for axis, bit in enumerate((core, chip % 2, chip // 2 % 2, chip // 4)):
            blocks = jnp.where(bit == 1, jnp.flip(blocks, axis), blocks)
        return blocks.reshape(rows_.shape)

    stages = [
        [(i, i ^ bit) for i in range(n_dp)] for bit in (1, 2, 4, 8)
    ]
    xg = flip(recv.reshape(rows, 2 * feat))
    x_rows, g_rows = xg[:, :feat], xg[:, feat:]

    def split(mul, left_rows, weight):
        return mul(left_rows[half:], weight).astype(BF), mul(left_rows[:half], weight)

    def reduce_scatter(mul, left_rows, weight):
        away, keep = split(mul, left_rows, weight)
        for n, perm in enumerate(stages):
            keep = lax.ppermute(away, "dp", perm).astype(F32) + keep.astype(F32)
            if n + 1 < len(stages):
                middle = keep.shape[0] // 2
                away, keep = keep[middle:].astype(BF), keep[:middle].astype(BF)
        return keep

    def all_gather(own):
        for perm in stages[::-1]:
            own = jnp.concatenate([own, lax.ppermute(own, "dp", perm)], axis=0)
        return own

    gu_gate, gu_up = gu[:, :width], gu[:, width:]
    gate = reduce_scatter(mm, x_rows, gu_gate)
    up = reduce_scatter(mm, x_rows, gu_up)
    hidden_grad = reduce_scatter(mm_nt, g_rows, down)
    sig = jax.nn.sigmoid(gate)
    silu_vals = gate * sig
    hidden = all_gather((silu_vals * up).astype(BF))
    dup = all_gather((hidden_grad * silu_vals).astype(BF))
    dgate = all_gather((hidden_grad * up * sig * (1.0 + gate * (1.0 - sig))).astype(BF))

    back = jnp.concatenate(
        [
            mm(hidden, down).astype(BF),
            (mm_nt(dgate, gu_gate) + mm_nt(dup, gu_up)).astype(BF),
        ],
        axis=1,
    )
    back = flip(back).reshape(experts, slots, 2 * feat)
    ret = lax.all_to_all(back, "expert", split_axis=0, concat_axis=0, tiled=True)
    ret = ret.reshape(rows, 2 * feat)
    grad_gu = mm_tn(x_rows, jnp.concatenate([dgate, dup], axis=1)).astype(BF)
    grad_dn = mm_tn(hidden, g_rows).astype(BF)

    mixed = sum(
        mm_tn(p.astype(BF), ret[:, :feat]) * route_weights[:, k : k + 1]
        for k, p in enumerate(picked)
    ).astype(BF)
    token_grad = mm_tn(selector, ret[:, feat:]).astype(BF)
    return (mixed, token_grad, grad_gu[None], grad_dn[None])


def solution(mesh):
    return jax.shard_map(
        on_device,
        mesh=mesh,
        in_specs=(
            P("expert", "dp"),
            P("expert", None),
            P("expert", None),
            P("expert", "dp"),
            P("expert", "dp", None),
            P("expert", None, "dp"),
        ),
        out_specs=(
            P("expert", "dp"),
            P("expert", "dp"),
            P("expert", "dp", None),
            P("expert", None, "dp"),
        ),
        check_vma=False,
    )
```

```python
import jax
import jax.numpy as jnp
from jax import lax
from jax.sharding import PartitionSpec as P

BF = jnp.bfloat16
F32 = jnp.float32


def mm(a, b):
    return jnp.dot(a, b, preferred_element_type=F32)


def mm_nt(a, b):
    return lax.dot_general(a, b, (((1,), (1,)), ((), ())), preferred_element_type=F32)


def mm_tn(a, b):
    return lax.dot_general(a, b, (((0,), (0,)), ((), ())), preferred_element_type=F32)


def route_slots(routes_t, experts, slots):
    top, count = routes_t.shape
    ids = lax.broadcasted_iota(jnp.int32, (experts, count), 0)
    earlier = lax.broadcasted_iota(jnp.int32, (count, count), 0) < lax.broadcasted_iota(
        jnp.int32, (count, count), 1
    )
    earlier = earlier.astype(BF)
    before = jnp.zeros((experts, 1), F32)
    targets = []
    for k in range(top):
        named = ids == routes_t[k : k + 1]
        hot = named.astype(BF)
        rank = mm(hot, earlier) + before
        slot = jnp.sum(jnp.where(named, rank, 0.0), axis=0, keepdims=True)
        targets.append(routes_t[k : k + 1] * slots + slot.astype(jnp.int32))
        before = before + jnp.sum(hot.astype(F32), axis=1, keepdims=True)
    return targets


def on_device(tokens, routes, route_weights, cotangent, w_gate_up, w_down):
    experts = lax.axis_size("expert")
    n_dp = lax.axis_size("dp")
    chips = n_dp // 2
    tok_rows, feat = tokens.shape
    top = routes.shape[1]
    width = w_down.shape[1]
    slots = 2 * tok_rows * top // experts
    rows = experts * slots
    half = rows // 2
    step = half // chips
    me = lax.axis_index("dp")
    chip = me // 2
    core = me % 2
    gu = w_gate_up[0]
    down = w_down[0]

    targets = route_slots(routes.T, experts, slots)
    weights = route_weights.T
    slot_ids = lax.broadcasted_iota(jnp.int32, (rows, tok_rows), 0)
    picked = [slot_ids == target for target in targets]
    selector = sum(p.astype(BF) for p in picked)
    slot_weight = sum(
        jnp.sum(jnp.where(p, weights[k : k + 1], 0.0), axis=1, keepdims=True)
        for k, p in enumerate(picked)
    )
    columns = lax.broadcasted_iota(jnp.int32, (rows, 2 * feat), 1)
    scale = jnp.where(columns < feat, 1.0, slot_weight)
    send = mm(selector, jnp.concatenate([tokens, cotangent], axis=1)) * scale
    send = send.astype(BF).reshape(experts, slots, 2 * feat)
    recv = lax.all_to_all(send, "expert", split_axis=0, concat_axis=0, tiled=True)

    def flip(rows_):
        blocks = rows_.reshape((2, 2, 2, 2, step) + rows_.shape[1:])
        for axis, bit in enumerate((core, chip % 2, chip // 2 % 2, chip // 4)):
            blocks = jnp.where(bit == 1, jnp.flip(blocks, axis), blocks)
        return blocks.reshape(rows_.shape)

    stages = [
        [(i, i ^ bit) for i in range(n_dp)] for bit in (1, 2, 4, 8)
    ]
    xg = flip(recv.reshape(rows, 2 * feat))
    x_rows, g_rows = xg[:, :feat], xg[:, feat:]

    def split(mul, left_rows, weight):
        return mul(left_rows[half:], weight).astype(BF), mul(left_rows[:half], weight)

    def reduce_scatter(mul, left_rows, weight):
        away, keep = split(mul, left_rows, weight)
        for n, perm in enumerate(stages):
            keep = lax.ppermute(away, "dp", perm).astype(F32) + keep.astype(F32)
            if n + 1 < len(stages):
                middle = keep.shape[0] // 2
                away, keep = keep[middle:].astype(BF), keep[:middle].astype(BF)
        return keep

    def all_gather(own):
        for perm in stages[::-1]:
            own = jnp.concatenate([own, lax.ppermute(own, "dp", perm)], axis=0)
        return own

    gu_gate, gu_up = gu[:, :width], gu[:, width:]
    gate = reduce_scatter(mm, x_rows, gu_gate)
    up = reduce_scatter(mm, x_rows, gu_up)
    hidden_grad = reduce_scatter(mm_nt, g_rows, down)
    sig = jax.nn.sigmoid(gate)
    silu_vals = gate * sig
    hidden = all_gather((silu_vals * up).astype(BF))
    dup = all_gather((hidden_grad * silu_vals).astype(BF))
    dgate = all_gather((hidden_grad * up * sig * (1.0 + gate * (1.0 - sig))).astype(BF))

    back = jnp.concatenate(
        [
            mm(hidden, down).astype(BF),
            (mm_nt(dgate, gu_gate) + mm_nt(dup, gu_up)).astype(BF),
        ],
        axis=1,
    )
    back = flip(back).reshape(experts, slots, 2 * feat)
    ret = lax.all_to_all(back, "expert", split_axis=0, concat_axis=0, tiled=True)
    ret = ret.reshape(rows, 2 * feat)
    grad_gu = mm_tn(x_rows, jnp.concatenate([dgate, dup], axis=1)).astype(BF)
    grad_dn = mm_tn(hidden, g_rows).astype(BF)

    mixed = sum(
        mm_tn(p.astype(BF), ret[:, :feat]) * route_weights[:, k : k + 1]
        for k, p in enumerate(picked)
    ).astype(BF)
    token_grad = mm_tn(selector, ret[:, feat:]).astype(BF)
    return (mixed, token_grad, grad_gu[None], grad_dn[None])


def solution(mesh):
    return jax.shard_map(
        on_device,
        mesh=mesh,
        in_specs=(
            P("expert", "dp"),
            P("expert", None),
            P("expert", None),
            P("expert", "dp"),
            P("expert", "dp", None),
            P("expert", None, "dp"),
        ),
        out_specs=(
            P("expert", "dp"),
            P("expert", "dp"),
            P("expert", "dp", None),
            P("expert", None, "dp"),
        ),
        check_vma=False,
    )
```
